32 devices in a mesh: row: 4 (over y, core), col: 8 (over z, x).
Axes of the slice: x: 2, y: 2, z: 4, core: 2. Of those that a mesh axis runs over, the one named last changes fastest.
Arguments:
- trailing_adjoint: float32 [1536, 1536], P('row', 'col'), may hold values from -3 to 3, as said below
- panel: float32 [1536, 256], P(('row', 'col')), may hold values from -0.15625 to 0.15625
- panel_adjoint: float32 [1536, 256], P(('row', 'col')), may hold values from -6 to 6
- diag_factor: float32 [256, 256], replicated, may hold values from -1 to 2, as said below
- diag_adjoint: float32 [256, 256], P('row', 'col'), may hold values from -6 to 6
Outputs:
- off_adjoint: float32 [1536, 256], P(('row', 'col'))
- block_adjoint: float32 [256, 256], replicated
The draws below stay inside these ranges and needn't reach their ends.
Inputs may be any that keep to these rules, and one draw needn't show every extreme that they name: `trailing_adjoint`: symmetric. `diag_factor`: lower triangular with diagonal entries from 1 to 2.
All inputs are finite; a program needn't handle non-finite values.
Results may differ from the reference program's by a relative error of at most 0.000071.
Values sent between devices are 32-bit elements; how exact they have to be, the bound alone decides.
A program may use at most 64 MiB of HBM per device.

```python
import math
import jax
import jax.numpy as jnp
from jax import lax

B = 256
N = 1536


def draw_trailing_adjoint(key, part):
    raw = jnp.clip(jax.random.normal(key, (N, N), jnp.float32), -4.0, 4.0)
    return (raw + raw.T) * 0.35


def draw_diag_factor(key, part):
    first = jax.random.fold_in(key, 11)
    second = jax.random.fold_in(key, 23)
    diagonal = jax.random.uniform(first, (B,), jnp.float32, 1.0, 2.0)
    spread = jnp.clip(jax.random.normal(second, (B, B), jnp.float32), -4.0, 4.0)
    lower = jnp.tril(spread, -1) * (0.3 / math.sqrt(B))
    return lower + jnp.diag(diagonal)


def level_of(rng, shape, pieces, least, high):
    factor_of = 1.0
    for position, blocks in pieces:
        heights = jax.random.uniform(jax.random.fold_in(jax.random.fold_in(rng, 6), position), (blocks,), jnp.float32, least / len(pieces), high / len(pieces))
        factor_of = factor_of * jnp.repeat(jnp.exp(heights), shape[position] // blocks).reshape((-1,) + (1,) * (len(shape) - 1 - position))
    return factor_of


def scatter_about(rng, dims, scale, reach, split=(), held_as=jnp.bfloat16):
    level = level_of(rng, dims, split, -0.22, 0.18) if split else 1.0
    values = jax.random.normal(rng, dims, jnp.float32) * scale * level
    return jnp.minimum(jnp.maximum(values, -reach), reach).astype(held_as)


def setup_inputs(seed: int = 0) -> dict:
    arg_keys = jax.random.split(jax.random.key(seed), 6)
    trailing_adjoint = draw_trailing_adjoint(jax.random.fold_in(arg_keys[5], 71), 0)
    panel = scatter_about(arg_keys[1], (N, B), N ** -0.5, 0.15625, ((0, 32),), jnp.float32)
    panel_adjoint = scatter_about(arg_keys[2], (N, B), 1.0, 6.0, ((0, 32),), jnp.float32)
    diag_factor = draw_diag_factor(jax.random.fold_in(arg_keys[5], 71), 0)
    diag_adjoint = scatter_about(arg_keys[4], (B, B), 1.0, 6.0, ((0, 4), (1, 8)), jnp.float32)
    return {"trailing_adjoint": trailing_adjoint, "panel": panel, "panel_adjoint": panel_adjoint, "diag_factor": diag_factor, "diag_adjoint": diag_adjoint}


def right_solve(factor, rows):
    return jax.scipy.linalg.solve_triangular(factor, rows.T, lower=True, trans=1).T

def left_solve(factor, matrix):
    return jax.scipy.linalg.solve_triangular(factor, matrix, lower=True, trans=1)

def diagonal_adjoint(factor, adjoint):
    product = jnp.dot(factor.T.astype(jnp.float32), adjoint.astype(jnp.float32), precision=lax.Precision.HIGHEST, preferred_element_type=jnp.float32)
    lower = jnp.tril(product) - 0.5 * jnp.diag(jnp.diag(product))
    symmetric = lower + lower.T
    half = left_solve(factor, symmetric)
    return 0.5 * left_solve(factor, half.T).T

def reference(trailing_adjoint, panel, panel_adjoint, diag_factor, diag_adjoint):
    product = jnp.dot(trailing_adjoint.astype(jnp.float32), panel.astype(jnp.float32), precision=lax.Precision.HIGHEST, preferred_element_type=jnp.float32)
    updated = panel_adjoint - 2.0 * product
    off_adjoint = right_solve(diag_factor, updated)
    contribution = jnp.dot(off_adjoint.T.astype(jnp.float32), panel.astype(jnp.float32), precision=lax.Precision.HIGHEST, preferred_element_type=jnp.float32)
    accumulated = diag_adjoint - contribution
    return (off_adjoint, diagonal_adjoint(diag_factor, accumulated))
```

```python
import functools

import jax
import jax.numpy as jnp
from jax import lax
from jax.experimental import pallas as pl
from jax.experimental.pallas import tpu as pltpu
from jax.sharding import PartitionSpec as P

MESH = pl.DeviceIdType.MESH
HIGHEST = lax.Precision.HIGHEST
CHUNK = 384


def dot(a, b):
    return jnp.dot(a, b, precision=HIGHEST, preferred_element_type=jnp.float32)


def tdot(a, b):
    return lax.dot_general(
        a, b, (((0,), (0,)), ((), ())), precision=HIGHEST, preferred_element_type=jnp.float32
    )


def iotas(shape):
    return (
        lax.broadcasted_iota(jnp.int32, shape, 0),
        lax.broadcasted_iota(jnp.int32, shape, 1),
    )


def inverse_pair(first, second):
    size = first.shape[0]
    i, j = iotas(first.shape)
    blocks, inverses = (first, second), []
    for block in blocks:
        diagonal = jnp.where(i == j, block, 0.0)
        down = 1.0 / jnp.sum(diagonal, axis=1, keepdims=True)
        across = 1.0 / jnp.sum(diagonal, axis=0, keepdims=True)
        pair = ((i >> 1) == (j >> 1)) & (i > j)
        inverses.append(
            jnp.where(i == j, jnp.broadcast_to(down, block.shape), 0.0)
            - jnp.where(pair, block, 0.0) * down * across
        )
    level = 1
    while (1 << level) < size:
        below = ((i >> (level + 1)) == (j >> (level + 1))) & ((i >> level) > (j >> level))
        halves = [dot(x, jnp.where(below, block, 0.0)) for x, block in zip(inverses, blocks)]
        inverses = [x - dot(half, x) for x, half in zip(inverses, halves)]
        level += 1
    return inverses


def wait_bytes(ref, semaphore):
    pltpu.make_async_copy(ref, ref, semaphore).wait()


def kernel(
    nrows, ncols, a_ref, p_ref, pa_ref, l_ref, d_ref, x_ref, k_ref,
    pbuf, tbuf, ubuf, wsend, wrecv, wfull, ebuf, linv,
    send_p, recv_row, recv_col, send_t, recv_t, send_w, recv_w, send_g, recv_g, send_e, recv_e,
):
    row, col = lax.axis_index("row"), lax.axis_index("col")
    count = nrows * ncols
    me = row * ncols + col
    stretch, width = p_ref.shape
    half = width // 2

    barrier = pltpu.get_barrier_semaphore()

    def greet(k, carry):
        peer = lax.rem(me + k, count)
        pl.semaphore_signal(
            barrier, inc=1, device_id=(peer // ncols, lax.rem(peer, ncols)), device_id_type=MESH
        )
        return carry

    lax.fori_loop(1, count, greet, 0)

    i, j = iotas((d_ref.shape[1], width))
    placed = dot(d_ref[...], jnp.where(j == i + col * d_ref.shape[1], 1.0, 0.0))
    drows = d_ref.shape[0]
    lrows = l_ref[pl.ds(pl.multiple_of(row * drows, drows), drows), :]
    wsend[...] = tdot(lrows, placed) - tdot(pa_ref[...], p_ref[...])
    pbuf[pl.ds(pl.multiple_of(col * stretch, stretch), stretch), :] = p_ref[...]

    pl.semaphore_wait(barrier, count - 1)

    home = me // nrows

    def to_row(k, carry):
        pltpu.make_async_remote_copy(
            src_ref=p_ref,
            dst_ref=pbuf.at[pl.ds(pl.multiple_of(col * stretch, stretch), stretch)],
            send_sem=send_p,
            recv_sem=recv_row,
            device_id=(row, lax.rem(col + k, ncols)),
            device_id_type=MESH,
        ).start()
        return carry

    def to_column(k, carry):
        slot = (ncols + lax.rem(me, nrows)) * stretch
        pltpu.make_async_remote_copy(
            src_ref=p_ref,
            dst_ref=pbuf.at[pl.ds(pl.multiple_of(slot, stretch), stretch)],
            send_sem=send_p,
            recv_sem=recv_col,
            device_id=(lax.rem(row + k, nrows), home),
            device_id_type=MESH,
        ).start()
        return carry

    lax.fori_loop(1, ncols, to_row, 0)
    lax.fori_loop(1, nrows, to_column, 0)

    low, high = inverse_pair(l_ref[:half, :half], l_ref[half:, half:])
    linv[:half, :half] = low
    linv[:half, half:] = jnp.zeros((half, half), jnp.float32)
    linv[half:, half:] = high
    linv[half:, :half] = -dot(high, dot(l_ref[half:, :half], low))

    wait_bytes(pbuf.at[pl.ds(0, (ncols - 1) * stretch)], recv_row)
    rows = a_ref.shape[0]
    tbuf[...] = tdot(a_ref[:CHUNK, :], pbuf[:CHUNK, :])
    if rows > CHUNK:

        def add_chunk(k, carry):
            part = pl.ds(pl.multiple_of(k * CHUNK, CHUNK), CHUNK)
            tbuf[...] += tdot(a_ref[part, :], pbuf[part, :])
            return carry

        lax.fori_loop(1, rows // CHUNK, add_chunk, 0)

    inside = row == (nrows * col) // ncols

    @pl.when(jnp.logical_not(inside))
    def _():
        wait_bytes(pbuf.at[pl.ds(0, nrows * stretch)], recv_col)

    base = jnp.where(inside, lax.rem(nrows * col, ncols), ncols) * stretch
    column_rows = pbuf[pl.ds(pl.multiple_of(base, stretch), nrows * stretch), :]
    wsend[...] += 2.0 * tdot(tbuf[...], column_rows)

    direct = count * 8 <= width
    group = count if direct else ncols
    place = me if direct else col
    piece = width // group

    def device_of(q):
        return (q // ncols, lax.rem(q, ncols)) if direct else (row, q)

    def scatter(k, carry):
        q = lax.rem(place + k, group)
        pltpu.make_async_remote_copy(
            src_ref=wsend.at[pl.ds(pl.multiple_of(q * piece, piece), piece)],
            dst_ref=wrecv.at[k - 1],
            send_sem=send_w,
            recv_sem=recv_w,
            device_id=device_of(q),
            device_id_type=MESH,
        ).start()
        return carry

    lax.fori_loop(1, group, scatter, 0)

    own = home == col
    for k in range(nrows):
        owner = nrows * col + k
        part = tbuf.at[pl.ds(k * stretch, stretch)]

        @pl.when(owner != me)
        def _():
            pltpu.make_async_remote_copy(
                src_ref=part,
                dst_ref=ubuf.at[row],
                send_sem=send_t,
                recv_sem=recv_t,
                device_id=(owner // ncols, lax.rem(owner, ncols)),
                device_id_type=MESH,
            ).start()

        @pl.when(owner == me)
        def _():
            ubuf[row] = part[...]

    mine = pl.ds(pl.multiple_of(place * piece, piece), piece)
    wait_bytes(wrecv, recv_w)
    total = wsend[mine, :] + jnp.sum(wrecv[...], axis=0)
    if not direct:
        ebuf[row] = total

        def exchange(k, carry):
            pltpu.make_async_remote_copy(
                src_ref=ebuf.at[row],
                dst_ref=ebuf.at[row],
                send_sem=send_e,
                recv_sem=recv_e,
                device_id=(lax.rem(row + k, nrows), col),
                device_id_type=MESH,
            ).start()
            return carry

        lax.fori_loop(1, nrows, exchange, 0)
        wait_bytes(ebuf.at[pl.ds(0, nrows - 1)], recv_e)
        total = jnp.sum(ebuf[...], axis=0)
    wfull[mine, :] = total

    def gather(k, carry):
        pltpu.make_async_remote_copy(
            src_ref=wfull.at[mine],
            dst_ref=wfull.at[mine],
            send_sem=send_g,
            recv_sem=recv_g,
            device_id=device_of(lax.rem(place + k, group)),
            device_id_type=MESH,
        ).start()
        return carry

    lax.fori_loop(1, group, gather, 0)

    @pl.when(own)
    def _():
        wait_bytes(ubuf.at[pl.ds(0, nrows - 1)], recv_t)
        wait_bytes(ubuf.at[pl.ds(0, nrows - 1)], send_t)

    @pl.when(jnp.logical_not(own))
    def _():
        wait_bytes(ubuf, recv_t)
        wait_bytes(ubuf, send_t)

    x_ref[...] = dot(pa_ref[...] - 2.0 * jnp.sum(ubuf[...], axis=0), linv[...])

    wait_bytes(wfull.at[pl.ds(0, (group - 1) * piece)], recv_g)
    w = wfull[...]
    i, j = iotas(w.shape)
    lower = jnp.where(i > j, w, jnp.where(i == j, 0.5 * w, 0.0))
    symmetric = lower + lower.T
    k_ref[...] = 0.5 * tdot(linv[...], dot(symmetric, linv[...]))

    wait_bytes(pbuf.at[pl.ds(0, (ncols + nrows - 2) * stretch)], send_p)
    wait_bytes(wrecv, send_w)
    wait_bytes(wfull.at[pl.ds(0, (group - 1) * piece)], send_g)
    if not direct:
        wait_bytes(ebuf.at[pl.ds(0, nrows - 1)], send_e)


def body(trailing_adjoint, panel, panel_adjoint, diag_factor, diag_adjoint):
    nrows, ncols = lax.axis_size("row"), lax.axis_size("col")
    stretch, width = panel.shape
    group = nrows * ncols if nrows * ncols * 8 <= width else ncols
    piece = width // group
    vmem = lambda *shape: pltpu.VMEM(shape, jnp.float32)
    return pl.pallas_call(
        functools.partial(kernel, nrows, ncols),
        out_shape=(
            jax.ShapeDtypeStruct(panel.shape, jnp.float32),
            jax.ShapeDtypeStruct(diag_factor.shape, jnp.float32),
        ),
        in_specs=[pl.BlockSpec(memory_space=pltpu.VMEM)] * 5,
        out_specs=(pl.BlockSpec(memory_space=pltpu.VMEM),) * 2,
        scratch_shapes=[
            vmem((ncols + nrows) * stretch, width),
            vmem(nrows * stretch, width),
            vmem(nrows, stretch, width),
            vmem(width, width),
            vmem(group - 1, piece, width),
            vmem(width, width),
            vmem(nrows, piece, width),
            vmem(width, width),
        ]
        + [pltpu.SemaphoreType.DMA] * 11,
        compiler_params=pltpu.CompilerParams(
            collective_id=0, has_side_effects=True, vmem_limit_bytes=40 * 1024 * 1024
        ),
    )(trailing_adjoint, panel, panel_adjoint, diag_factor, diag_adjoint)


def solution(mesh):
    return jax.shard_map(
        body,
        mesh=mesh,
        in_specs=(
            P("row", "col"),
            P(("row", "col"), None),
            P(("row", "col"), None),
            P(),
            P("row", "col"),
        ),
        out_specs=(P(("row", "col"), None), P()),
        check_vma=False,
    )
```

```python
import functools

import jax
import jax.numpy as jnp
from jax import lax
from jax.experimental import pallas as pl
from jax.experimental.pallas import tpu as pltpu
from jax.sharding import PartitionSpec as P

MESH = pl.DeviceIdType.MESH
HIGHEST = lax.Precision.HIGHEST
CHUNK = 384


def split(x):
    high = x.astype(jnp.bfloat16)
    return high, (x - high.astype(jnp.float32)).astype(jnp.bfloat16)


def one(a, b):
    return jnp.dot(a, b, preferred_element_type=jnp.float32)


def dot_parts(a, b):
    return one(a[0], b[0]) + (one(a[0], b[1]) + one(a[1], b[0]))


def dot(a, b):
    return dot_parts(split(a), split(b))


def tdot(a, b):
    return dot(a.T, b)


def exact_dot(a, b):
    return jnp.dot(a, b, precision=HIGHEST, preferred_element_type=jnp.float32)


def iotas(shape):
    return (
        lax.broadcasted_iota(jnp.int32, shape, 0),
        lax.broadcasted_iota(jnp.int32, shape, 1),
    )


def inverse_pair(first, second):
    size = first.shape[0]
    i, j = iotas(first.shape)
    blocks, inverses = (first, second), []
    for block in blocks:
        diagonal = jnp.where(i == j, block, 0.0)
        down = 1.0 / jnp.sum(diagonal, axis=1, keepdims=True)
        across = 1.0 / jnp.sum(diagonal, axis=0, keepdims=True)
        pair = ((i >> 1) == (j >> 1)) & (i > j)
        inverses.append(
            jnp.where(i == j, jnp.broadcast_to(down, block.shape), 0.0)
            - jnp.where(pair, block, 0.0) * down * across
        )
    level = 1
    while (1 << level) < size:
        below = ((i >> (level + 1)) == (j >> (level + 1))) & ((i >> level) > (j >> level))
        halves = [dot(x, jnp.where(below, block, 0.0)) for x, block in zip(inverses, blocks)]
        inverses = [x - dot(half, x) for x, half in zip(inverses, halves)]
        level += 1
    return inverses


def wait_bytes(ref, semaphore):
    pltpu.make_async_copy(ref, ref, semaphore).wait()


def kernel(
    nrows, ncols, a_ref, p_ref, pa_ref, l_ref, d_ref, x_ref, k_ref,
    pbuf, tbuf, ubuf, sbuf, fsend, fbuf, wsend, wrecv, wfull, ebuf, linv, linv_t,
    send_p, recv_row, recv_col, send_t, recv_t, send_w, recv_w, send_g, recv_g, send_e, recv_e,
    send_s, recv_s, send_f, recv_f,
):
    row, col = lax.axis_index("row"), lax.axis_index("col")
    count = nrows * ncols
    me = row * ncols + col
    stretch, width = p_ref.shape
    half = width // 2

    barrier = pltpu.get_barrier_semaphore()

    def greet(k, carry):
        peer = lax.rem(me + k, count)
        pl.semaphore_signal(
            barrier, inc=1, device_id=(peer // ncols, lax.rem(peer, ncols)), device_id_type=MESH
        )
        return carry

    lax.fori_loop(1, count, greet, 0)

    i, j = iotas((d_ref.shape[0], width))
    placed = tdot(d_ref[...], jnp.where(j == i + col * d_ref.shape[0], 1.0, 0.0))
    drows = d_ref.shape[1]
    lrows = l_ref[pl.ds(pl.multiple_of(row * drows, drows), drows), :]
    wsend[...] = tdot(lrows, placed) - tdot(pa_ref[...], p_ref[...])
    pbuf[pl.ds(pl.multiple_of(col * stretch, stretch), stretch), :] = p_ref[...]

    pl.semaphore_wait(barrier, count - 1)

    shard = pl.ds(pl.multiple_of(col * stretch, stretch), stretch)
    fours = ncols // 2
    place_c, parity = col // 2, lax.rem(col, 2)
    neighbour = 2 * place_c + 1 - parity
    summer = (lax.rem(me, nrows), me // nrows)
    owner = nrows * col + row
    fixed = owner == me

    def to_row(k, carry):
        pltpu.make_async_remote_copy(
            src_ref=p_ref,
            dst_ref=pbuf.at[shard],
            send_sem=send_p,
            recv_sem=recv_row.at[k],
            device_id=(row, 2 * lax.rem(place_c + k, fours) + parity),
            device_id_type=MESH,
        ).start()
        return carry

    lax.fori_loop(1, fours, to_row, 0)
    pltpu.make_async_remote_copy(
        src_ref=p_ref, dst_ref=pbuf.at[shard], send_sem=send_p, recv_sem=recv_col,
        device_id=(row, neighbour), device_id_type=MESH,
    ).start()

    def hand_on(k, carry):
        origin = 2 * lax.rem(place_c + fours - k, fours) + parity
        arrived = pbuf.at[pl.ds(pl.multiple_of(origin * stretch, stretch), stretch)]
        wait_bytes(arrived, recv_row.at[k])
        pltpu.make_async_remote_copy(
            src_ref=arrived, dst_ref=arrived, send_sem=send_p, recv_sem=recv_col,
            device_id=(row, neighbour), device_id_type=MESH,
        ).start()
        return carry

    lax.fori_loop(1, fours, hand_on, 0)

    @pl.when(jnp.logical_not(fixed))
    def _():
        pltpu.make_async_remote_copy(
            src_ref=p_ref, dst_ref=sbuf, send_sem=send_s, recv_sem=recv_s,
            device_id=summer, device_id_type=MESH,
        ).start()

    @pl.when(fixed)
    def _():
        sbuf[...] = p_ref[...]

    wait_bytes(pbuf.at[pl.ds(0, fours * stretch)], recv_col)
    rows = a_ref.shape[1]
    tbuf[...] = dot(a_ref[:, :CHUNK], pbuf[:CHUNK, :])
    if rows > CHUNK:

        def add_chunk(k, carry):
            part = pl.ds(pl.multiple_of(k * CHUNK, CHUNK), CHUNK)
            tbuf[...] += dot(a_ref[:, part], pbuf[part, :])
            return carry

        lax.fori_loop(1, rows // CHUNK, add_chunk, 0)

    def to_summer(k, carry):
        q = lax.rem(row + k, nrows)
        pltpu.make_async_remote_copy(
            src_ref=tbuf.at[pl.ds(pl.multiple_of(q * stretch, stretch), stretch)],
            dst_ref=ubuf.at[k - 1],
            send_sem=send_t,
            recv_sem=recv_t,
            device_id=(q, col),
            device_id_type=MESH,
        ).start()
        return carry

    lax.fori_loop(1, nrows, to_summer, 0)
    low, high = inverse_pair(l_ref[:half, :half], l_ref[half:, half:])
    linv[:half, :half] = low
    linv[:half, half:] = jnp.zeros((half, half), jnp.float32)
    linv[half:, half:] = high
    linv[half:, :half] = -dot(high, dot(l_ref[half:, :half], low))

    linv_t[...] = linv[...].T

    wait_bytes(ubuf, recv_t)
    mine = pl.ds(pl.multiple_of(row * stretch, stretch), stretch)
    fsend[...] = tbuf[mine, :] + jnp.sum(ubuf[...], axis=0)

    @pl.when(jnp.logical_not(fixed))
    def _():
        wait_bytes(sbuf, recv_s)

    wsend[...] += 2.0 * tdot(fsend[...], sbuf[...])

    direct = count * 8 <= width
    group = count if direct else ncols
    place = me if direct else col
    piece = width // group

    def device_of(q):
        return (q // ncols, lax.rem(q, ncols)) if direct else (row, q)

    def scatter(k, carry):
        q = lax.rem(place + k, group)
        pltpu.make_async_remote_copy(
            src_ref=wsend.at[pl.ds(pl.multiple_of(q * piece, piece), piece)],
            dst_ref=wrecv.at[k - 1],
            send_sem=send_w,
            recv_sem=recv_w,
            device_id=device_of(q),
            device_id_type=MESH,
        ).start()
        return carry

    lax.fori_loop(1, group, scatter, 0)

    @pl.when(jnp.logical_not(fixed))
    def _():
        pltpu.make_async_remote_copy(
            src_ref=fsend, dst_ref=fbuf, send_sem=send_f, recv_sem=recv_f,
            device_id=(owner // ncols, lax.rem(owner, ncols)), device_id_type=MESH,
        ).start()

    @pl.when(fixed)
    def _():
        fbuf[...] = fsend[...]

    mine = pl.ds(pl.multiple_of(place * piece, piece), piece)
    wait_bytes(wrecv, recv_w)
    total = wsend[mine, :] + jnp.sum(wrecv[...], axis=0)
    if not direct:
        ebuf[row] = total

        def exchange(k, carry):
            pltpu.make_async_remote_copy(
                src_ref=ebuf.at[row],
                dst_ref=ebuf.at[row],
                send_sem=send_e,
                recv_sem=recv_e,
                device_id=(lax.rem(row + k, nrows), col),
                device_id_type=MESH,
            ).start()
            return carry

        lax.fori_loop(1, nrows, exchange, 0)
        wait_bytes(ebuf.at[pl.ds(0, nrows - 1)], recv_e)
        total = jnp.sum(ebuf[...], axis=0)
    wfull[mine, :] = total

    def gather(k, carry):
        pltpu.make_async_remote_copy(
            src_ref=wfull.at[mine],
            dst_ref=wfull.at[mine],
            send_sem=send_g,
            recv_sem=recv_g,
            device_id=device_of(lax.rem(place + k, group)),
            device_id_type=MESH,
        ).start()
        return carry

    lax.fori_loop(1, group, gather, 0)

    @pl.when(jnp.logical_not(fixed))
    def _():
        wait_bytes(fbuf, recv_f)

    x_ref[...] = dot(pa_ref[...] - 2.0 * fbuf[...], linv[...])

    wait_bytes(wfull.at[pl.ds(0, (group - 1) * piece)], recv_g)
    w = wfull[...]
    i, j = iotas(w.shape)
    lower = jnp.where(i > j, w, jnp.where(i == j, 0.5 * w, 0.0))
    symmetric = lower + lower.T
    inverse = split(linv[...])
    right = dot_parts(split(symmetric), inverse)
    k_ref[...] = 0.5 * dot_parts(split(linv_t[...]), split(right))

    wait_bytes(pbuf.at[pl.ds(0, (ncols - 1) * stretch)], send_p)
    wait_bytes(ubuf, send_t)

    @pl.when(jnp.logical_not(fixed))
    def _():
        wait_bytes(sbuf, send_s)
        wait_bytes(fbuf, send_f)

    wait_bytes(wrecv, send_w)
    wait_bytes(wfull.at[pl.ds(0, (group - 1) * piece)], send_g)
    if not direct:
        wait_bytes(ebuf.at[pl.ds(0, nrows - 1)], send_e)


def body(trailing_adjoint, panel, panel_adjoint, diag_factor, diag_adjoint):
    nrows, ncols = lax.axis_size("row"), lax.axis_size("col")
    stretch, width = panel.shape
    group = nrows * ncols if nrows * ncols * 8 <= width else ncols
    piece = width // group
    vmem = lambda *shape: pltpu.VMEM(shape, jnp.float32)
    return pl.pallas_call(
        functools.partial(kernel, nrows, ncols),
        out_shape=(
            jax.ShapeDtypeStruct(panel.shape, jnp.float32),
            jax.ShapeDtypeStruct(diag_factor.shape, jnp.float32),
        ),
        in_specs=[pl.BlockSpec(memory_space=pltpu.VMEM)] * 5,
        out_specs=(pl.BlockSpec(memory_space=pltpu.VMEM),) * 2,
        scratch_shapes=[
            vmem(ncols * stretch, width),
            vmem(nrows * stretch, width),
            vmem(nrows - 1, stretch, width),
            vmem(stretch, width),
            vmem(stretch, width),
            vmem(stretch, width),
            vmem(width, width),
            vmem(group - 1, piece, width),
            vmem(width, width),
            vmem(nrows, piece, width),
            vmem(width, width),
            vmem(width, width),
        ]
        + [pltpu.SemaphoreType.DMA, pltpu.SemaphoreType.DMA((ncols // 2,))]
        + [pltpu.SemaphoreType.DMA] * 13,
        compiler_params=pltpu.CompilerParams(
            collective_id=0, has_side_effects=True, vmem_limit_bytes=40 * 1024 * 1024
        ),
    )(trailing_adjoint.T, panel, panel_adjoint, diag_factor, diag_adjoint.T)


def solution(mesh):
    return jax.shard_map(
        body,
        mesh=mesh,
        in_specs=(
            P("row", "col"),
            P(("row", "col"), None),
            P(("row", "col"), None),
            P(),
            P("row", "col"),
        ),
        out_specs=(P(("row", "col"), None), P()),
        check_vma=False,
    )
```

```python
import functools

import jax
import jax.numpy as jnp
from jax import lax
from jax.experimental import pallas as pl
from jax.experimental.pallas import tpu as pltpu
from jax.sharding import PartitionSpec as P

MESH = pl.DeviceIdType.MESH
HIGHEST = lax.Precision.HIGHEST
CHUNK = 384


def split(x):
    high = x.astype(jnp.bfloat16)
    return high, (x - high.astype(jnp.float32)).astype(jnp.bfloat16)


def one(a, b):
    return jnp.dot(a, b, preferred_element_type=jnp.float32)


def dot_parts(a, b):
    return one(a[0], b[0]) + (one(a[0], b[1]) + one(a[1], b[0]))


def dot(a, b):
    return dot_parts(split(a), split(b))


def tdot(a, b):
    return dot(a.T, b)


def exact_dot(a, b):
    return jnp.dot(a, b, precision=HIGHEST, preferred_element_type=jnp.float32)


def iotas(shape):
    return (
        lax.broadcasted_iota(jnp.int32, shape, 0),
        lax.broadcasted_iota(jnp.int32, shape, 1),
    )


def inverse_pair(first, second):
    size = first.shape[0]
    i, j = iotas(first.shape)
    blocks, inverses = (first, second), []
    for block in blocks:
        diagonal = jnp.where(i == j, block, 0.0)
        down = 1.0 / jnp.sum(diagonal, axis=1, keepdims=True)
        across = 1.0 / jnp.sum(diagonal, axis=0, keepdims=True)
        pair = ((i >> 1) == (j >> 1)) & (i > j)
        inverses.append(
            jnp.where(i == j, jnp.broadcast_to(down, block.shape), 0.0)
            - jnp.where(pair, block, 0.0) * down * across
        )
    level = 1
    while (1 << level) < size:
        below = ((i >> (level + 1)) == (j >> (level + 1))) & ((i >> level) > (j >> level))
        halves = [dot(x, jnp.where(below, block, 0.0)) for x, block in zip(inverses, blocks)]
        inverses = [x - dot(half, x) for x, half in zip(inverses, halves)]
        level += 1
    return inverses


def wait_bytes(ref, semaphore):
    pltpu.make_async_copy(ref, ref, semaphore).wait()


def kernel(
    nrows, ncols, a_ref, p_ref, pa_ref, l_ref, d_ref, x_ref, k_ref,
    pbuf, tbuf, ubuf, sbuf, fsend, fbuf, wsend, wrecv, wfull, ebuf, linv, linv_t,
    send_p, recv_row, recv_col, send_t, recv_t, send_w, recv_w, send_g, recv_g, send_e, recv_e,
    send_s, recv_s, send_f, recv_f,
):
    row, col = lax.axis_index("row"), lax.axis_index("col")
    count = nrows * ncols
    me = row * ncols + col
    stretch, width = p_ref.shape
    half = width // 2

    barrier = pltpu.get_barrier_semaphore()

    def greet(k, carry):
        peer = lax.rem(me + k, count)
        pl.semaphore_signal(
            barrier, inc=1, device_id=(peer // ncols, lax.rem(peer, ncols)), device_id_type=MESH
        )
        return carry

    lax.fori_loop(1, count, greet, 0)

    i, j = iotas((d_ref.shape[0], width))
    placed = tdot(d_ref[...], jnp.where(j == i + col * d_ref.shape[0], 1.0, 0.0))
    drows = d_ref.shape[1]
    lrows = l_ref[pl.ds(pl.multiple_of(row * drows, drows), drows), :]
    wsend[...] = tdot(lrows, placed) - tdot(pa_ref[...], p_ref[...])
    pbuf[pl.ds(pl.multiple_of(col * stretch, stretch), stretch), :] = p_ref[...]

    pl.semaphore_wait(barrier, count - 1)

    shard = pl.ds(pl.multiple_of(col * stretch, stretch), stretch)
    fours = ncols // 2
    place_c, parity = col // 2, lax.rem(col, 2)
    neighbour = 2 * place_c + 1 - parity
    summer = (lax.rem(me, nrows), me // nrows)
    owner = nrows * col + row
    fixed = owner == me

    def to_row(k, carry):
        pltpu.make_async_remote_copy(
            src_ref=p_ref,
            dst_ref=pbuf.at[shard],
            send_sem=send_p,
            recv_sem=recv_row.at[k],
            device_id=(row, 2 * lax.rem(place_c + k, fours) + parity),
            device_id_type=MESH,
        ).start()
        return carry

    lax.fori_loop(1, fours, to_row, 0)
    pltpu.make_async_remote_copy(
        src_ref=p_ref, dst_ref=pbuf.at[shard], send_sem=send_p, recv_sem=recv_col,
        device_id=(row, neighbour), device_id_type=MESH,
    ).start()

    def hand_on(k, carry):
        origin = 2 * lax.rem(place_c + fours - k, fours) + parity
        arrived = pbuf.at[pl.ds(pl.multiple_of(origin * stretch, stretch), stretch)]
        wait_bytes(arrived, recv_row.at[k])
        pltpu.make_async_remote_copy(
            src_ref=arrived, dst_ref=arrived, send_sem=send_p, recv_sem=recv_col,
            device_id=(row, neighbour), device_id_type=MESH,
        ).start()
        return carry

    lax.fori_loop(1, fours, hand_on, 0)

    @pl.when(jnp.logical_not(fixed))
    def _():
        pltpu.make_async_remote_copy(
            src_ref=p_ref, dst_ref=sbuf, send_sem=send_s, recv_sem=recv_s,
            device_id=summer, device_id_type=MESH,
        ).start()

    @pl.when(fixed)
    def _():
        sbuf[...] = p_ref[...]

    wait_bytes(pbuf.at[pl.ds(0, fours * stretch)], recv_col)
    rows = a_ref.shape[1]
    tbuf[...] = dot(a_ref[:, :CHUNK], pbuf[:CHUNK, :])
    if rows > CHUNK:

        def add_chunk(k, carry):
            part = pl.ds(pl.multiple_of(k * CHUNK, CHUNK), CHUNK)
            tbuf[...] += dot(a_ref[:, part], pbuf[part, :])
            return carry

        lax.fori_loop(1, rows // CHUNK, add_chunk, 0)

    def to_summer(k, carry):
        q = lax.rem(row + k, nrows)
        pltpu.make_async_remote_copy(
            src_ref=tbuf.at[pl.ds(pl.multiple_of(q * stretch, stretch), stretch)],
            dst_ref=ubuf.at[k - 1],
            send_sem=send_t,
            recv_sem=recv_t,
            device_id=(q, col),
            device_id_type=MESH,
        ).start()
        return carry

    lax.fori_loop(1, nrows, to_summer, 0)
    low, high = inverse_pair(l_ref[:half, :half], l_ref[half:, half:])
    linv[:half, :half] = low
    linv[:half, half:] = jnp.zeros((half, half), jnp.float32)
    linv[half:, half:] = high
    linv[half:, :half] = -dot(high, dot(l_ref[half:, :half], low))

    linv_t[...] = linv[...].T

    wait_bytes(ubuf, recv_t)
    mine = pl.ds(pl.multiple_of(row * stretch, stretch), stretch)
    fsend[...] = tbuf[mine, :] + jnp.sum(ubuf[...], axis=0)

    @pl.when(jnp.logical_not(fixed))
    def _():
        wait_bytes(sbuf, recv_s)

    wsend[...] += 2.0 * tdot(fsend[...], sbuf[...])

    direct = count * 8 <= width
    group = count if direct else ncols
    place = me if direct else col
    piece = width // group

    def device_of(q):
        return (q // ncols, lax.rem(q, ncols)) if direct else (row, q)

    def scatter(k, carry):
        q = lax.rem(place + k, group)
        part = pl.ds(pl.multiple_of(q * piece, piece), piece)

        def send(columns):
            pltpu.make_async_remote_copy(
                src_ref=wsend.at[part, :columns],
                dst_ref=wrecv.at[k - 1, :, :columns],
                send_sem=send_w,
                recv_sem=recv_w,
                device_id=device_of(q),
                device_id_type=MESH,
            ).start()

        pl.when(q < group // 2)(lambda: send(half))
        pl.when(q >= group // 2)(lambda: send(width))
        return carry

    lax.fori_loop(1, group, scatter, 0)

    @pl.when(jnp.logical_not(fixed))
    def _():
        pltpu.make_async_remote_copy(
            src_ref=fsend, dst_ref=fbuf, send_sem=send_f, recv_sem=recv_f,
            device_id=(owner // ncols, lax.rem(owner, ncols)), device_id_type=MESH,
        ).start()

    @pl.when(fixed)
    def _():
        fbuf[...] = fsend[...]

    mine = pl.ds(pl.multiple_of(place * piece, piece), piece)
    upper = place < group // 2

    def others(semaphore):
        rows = width + half
        pl.when(upper)(lambda: wait_bytes(pbuf.at[: rows - piece, :half], semaphore))
        pl.when(jnp.logical_not(upper))(
            lambda: wait_bytes(pbuf.at[: rows - 2 * piece, :half], semaphore)
        )

    pl.when(upper)(lambda: wait_bytes(wrecv.at[:, :, :half], recv_w))
    pl.when(jnp.logical_not(upper))(lambda: wait_bytes(wrecv, recv_w))
    total = wsend[mine, :] + jnp.sum(wrecv[...], axis=0)
    if not direct:
        ebuf[row] = total

        def exchange(k, carry):
            pltpu.make_async_remote_copy(
                src_ref=ebuf.at[row],
                dst_ref=ebuf.at[row],
                send_sem=send_e,
                recv_sem=recv_e,
                device_id=(lax.rem(row + k, nrows), col),
                device_id_type=MESH,
            ).start()
            return carry

        lax.fori_loop(1, nrows, exchange, 0)
        wait_bytes(ebuf.at[pl.ds(0, nrows - 1)], recv_e)
        total = jnp.sum(ebuf[...], axis=0)
    wfull[mine, :] = total

    def gather(k, carry):
        def send(columns):
            pltpu.make_async_remote_copy(
                src_ref=wfull.at[mine, :columns],
                dst_ref=wfull.at[mine, :columns],
                send_sem=send_g,
                recv_sem=recv_g,
                device_id=device_of(lax.rem(place + k, group)),
                device_id_type=MESH,
            ).start()

        pl.when(upper)(lambda: send(half))
        pl.when(jnp.logical_not(upper))(lambda: send(width))
        return carry

    lax.fori_loop(1, group, gather, 0)

    @pl.when(jnp.logical_not(fixed))
    def _():
        wait_bytes(fbuf, recv_f)

    x_ref[...] = dot(pa_ref[...] - 2.0 * fbuf[...], linv[...])

    others(recv_g)
    wfull[:half, half:] = jnp.zeros((half, half), jnp.float32)
    w = wfull[...]
    i, j = iotas(w.shape)
    lower = jnp.where(i > j, w, jnp.where(i == j, 0.5 * w, 0.0))
    symmetric = lower + lower.T
    inverse = split(linv[...])
    right = dot_parts(split(symmetric), inverse)
    k_ref[...] = 0.5 * dot_parts(split(linv_t[...]), split(right))

    wait_bytes(pbuf.at[pl.ds(0, (ncols - 1) * stretch)], send_p)
    wait_bytes(ubuf, send_t)

    @pl.when(jnp.logical_not(fixed))
    def _():
        wait_bytes(sbuf, send_s)
        wait_bytes(fbuf, send_f)

    others(send_w)
    pl.when(upper)(lambda: wait_bytes(wrecv.at[:, :, :half], send_g))
    pl.when(jnp.logical_not(upper))(lambda: wait_bytes(wrecv, send_g))
    if not direct:
        wait_bytes(ebuf.at[pl.ds(0, nrows - 1)], send_e)


def body(trailing_adjoint, panel, panel_adjoint, diag_factor, diag_adjoint):
    nrows, ncols = lax.axis_size("row"), lax.axis_size("col")
    stretch, width = panel.shape
    group = nrows * ncols if nrows * ncols * 8 <= width else ncols
    piece = width // group
    vmem = lambda *shape: pltpu.VMEM(shape, jnp.float32)
    return pl.pallas_call(
        functools.partial(kernel, nrows, ncols),
        out_shape=(
            jax.ShapeDtypeStruct(panel.shape, jnp.float32),
            jax.ShapeDtypeStruct(diag_factor.shape, jnp.float32),
        ),
        in_specs=[pl.BlockSpec(memory_space=pltpu.VMEM)] * 5,
        out_specs=(pl.BlockSpec(memory_space=pltpu.VMEM),) * 2,
        scratch_shapes=[
            vmem(ncols * stretch, width),
            vmem(nrows * stretch, width),
            vmem(nrows - 1, stretch, width),
            vmem(stretch, width),
            vmem(stretch, width),
            vmem(stretch, width),
            vmem(width, width),
            vmem(group - 1, piece, width),
            vmem(width, width),
            vmem(nrows, piece, width),
            vmem(width, width),
            vmem(width, width),
        ]
        + [pltpu.SemaphoreType.DMA, pltpu.SemaphoreType.DMA((ncols // 2,))]
        + [pltpu.SemaphoreType.DMA] * 13,
        compiler_params=pltpu.CompilerParams(
            collective_id=0, has_side_effects=True, vmem_limit_bytes=40 * 1024 * 1024
        ),
    )(trailing_adjoint.T, panel, panel_adjoint, diag_factor, diag_adjoint.T)


def solution(mesh):
    return jax.shard_map(
        body,
        mesh=mesh,
        in_specs=(
            P("row", "col"),
            P(("row", "col"), None),
            P(("row", "col"), None),
            P(),
            P("row", "col"),
        ),
        out_specs=(P(("row", "col"), None), P()),
        check_vma=False,
    )
```

```python
import functools

import jax
import jax.numpy as jnp
from jax import lax
from jax.experimental import pallas as pl
from jax.experimental.pallas import tpu as pltpu
from jax.sharding import PartitionSpec as P

MESH = pl.DeviceIdType.MESH
HIGHEST = lax.Precision.HIGHEST
CHUNK = 384


def split(x):
    high = x.astype(jnp.bfloat16)
    return high, (x - high.astype(jnp.float32)).astype(jnp.bfloat16)


def one(a, b):
    return jnp.dot(a, b, preferred_element_type=jnp.float32)


def dot_parts(a, b):
    return one(a[0], b[0]) + (one(a[0], b[1]) + one(a[1], b[0]))


def dot(a, b):
    return dot_parts(split(a), split(b))


def tdot(a, b):
    return dot(a.T, b)


def exact_dot(a, b):
    return jnp.dot(a, b, precision=HIGHEST, preferred_element_type=jnp.float32)


def iotas(shape):
    return (
        lax.broadcasted_iota(jnp.int32, shape, 0),
        lax.broadcasted_iota(jnp.int32, shape, 1),
    )


def inverse_pair(first, second):
    size = first.shape[0]
    i, j = iotas(first.shape)
    blocks, inverses = (first, second), []
    for block in blocks:
        diagonal = jnp.where(i == j, block, 0.0)
        down = 1.0 / jnp.sum(diagonal, axis=1, keepdims=True)
        across = 1.0 / jnp.sum(diagonal, axis=0, keepdims=True)
        pair = ((i >> 1) == (j >> 1)) & (i > j)
        inverses.append(
            jnp.where(i == j, jnp.broadcast_to(down, block.shape), 0.0)
            - jnp.where(pair, block, 0.0) * down * across
        )
    level = 1
    while (1 << level) < size:
        below = ((i >> (level + 1)) == (j >> (level + 1))) & ((i >> level) > (j >> level))
        halves = [dot(x, jnp.where(below, block, 0.0)) for x, block in zip(inverses, blocks)]
        inverses = [x - dot(half, x) for x, half in zip(inverses, halves)]
        level += 1
    return inverses


def wait_bytes(ref, semaphore):
    pltpu.make_async_copy(ref, ref, semaphore).wait()


def kernel(
    nrows, ncols, a_ref, p_ref, pa_ref, l_ref, d_ref, x_ref, k_ref,
    pbuf, tbuf, ubuf, sbuf, fsend, fbuf, wsend, wrecv, wfull, ebuf, linv, linv_t,
    send_p, recv_row, recv_col, send_t, recv_t, send_w, recv_w, send_g, recv_g, send_e, recv_e,
    send_s, recv_s, send_f, recv_f,
):
    row, col = lax.axis_index("row"), lax.axis_index("col")
    count = nrows * ncols
    me = row * ncols + col
    stretch, width = p_ref.shape
    half = width // 2

    barrier = pltpu.get_barrier_semaphore()

    def greet(k, carry):
        peer = lax.rem(me + k, count)
        pl.semaphore_signal(
            barrier, inc=1, device_id=(peer // ncols, lax.rem(peer, ncols)), device_id_type=MESH
        )
        return carry

    lax.fori_loop(1, count, greet, 0)

    i, j = iotas((d_ref.shape[0], width))
    placed = tdot(d_ref[...], jnp.where(j == i + col * d_ref.shape[0], 1.0, 0.0))
    drows = d_ref.shape[1]
    lrows = l_ref[pl.ds(pl.multiple_of(row * drows, drows), drows), :]
    wsend[...] = tdot(lrows, placed) - tdot(pa_ref[...], p_ref[...])
    pbuf[pl.ds(pl.multiple_of(col * stretch, stretch), stretch), :] = p_ref[...]

    pl.semaphore_wait(barrier, count - 1)

    shard = pl.ds(pl.multiple_of(col * stretch, stretch), stretch)
    fours = ncols // 2
    place_c, parity = col // 2, lax.rem(col, 2)
    neighbour = 2 * place_c + 1 - parity
    summer = (lax.rem(me, nrows), me // nrows)
    owner = nrows * col + row
    fixed = owner == me

    def to_row(k, carry):
        pltpu.make_async_remote_copy(
            src_ref=p_ref,
            dst_ref=pbuf.at[shard],
            send_sem=send_p,
            recv_sem=recv_row.at[k],
            device_id=(row, 2 * lax.rem(place_c + k, fours) + parity),
            device_id_type=MESH,
        ).start()
        return carry

    lax.fori_loop(1, fours, to_row, 0)
    pltpu.make_async_remote_copy(
        src_ref=p_ref, dst_ref=pbuf.at[shard], send_sem=send_p, recv_sem=recv_col,
        device_id=(row, neighbour), device_id_type=MESH,
    ).start()

    def hand_on(k, carry):
        origin = 2 * lax.rem(place_c + fours - k, fours) + parity
        arrived = pbuf.at[pl.ds(pl.multiple_of(origin * stretch, stretch), stretch)]
        wait_bytes(arrived, recv_row.at[k])
        pltpu.make_async_remote_copy(
            src_ref=arrived, dst_ref=arrived, send_sem=send_p, recv_sem=recv_col,
            device_id=(row, neighbour), device_id_type=MESH,
        ).start()
        return carry

    lax.fori_loop(1, fours, hand_on, 0)

    @pl.when(jnp.logical_not(fixed))
    def _():
        pltpu.make_async_remote_copy(
            src_ref=p_ref, dst_ref=sbuf, send_sem=send_s, recv_sem=recv_s,
            device_id=summer, device_id_type=MESH,
        ).start()

    @pl.when(fixed)
    def _():
        sbuf[...] = p_ref[...]

    wait_bytes(pbuf.at[pl.ds(0, fours * stretch)], recv_col)
    rows = a_ref.shape[1]
    tbuf[...] = dot(a_ref[:, :CHUNK], pbuf[:CHUNK, :])
    if rows > CHUNK:

        def add_chunk(k, carry):
            part = pl.ds(pl.multiple_of(k * CHUNK, CHUNK), CHUNK)
            tbuf[...] += dot(a_ref[:, part], pbuf[part, :])
            return carry

        lax.fori_loop(1, rows // CHUNK, add_chunk, 0)

    def to_summer(k, carry):
        q = lax.rem(row + k, nrows)
        pltpu.make_async_remote_copy(
            src_ref=tbuf.at[pl.ds(pl.multiple_of(q * stretch, stretch), stretch)],
            dst_ref=ubuf.at[k - 1],
            send_sem=send_t,
            recv_sem=recv_t,
            device_id=(q, col),
            device_id_type=MESH,
        ).start()
        return carry

    lax.fori_loop(1, nrows, to_summer, 0)
    low, high = inverse_pair(l_ref[:half, :half], l_ref[half:, half:])
    linv[:half, :half] = low
    linv[:half, half:] = jnp.zeros((half, half), jnp.float32)
    linv[half:, half:] = high
    linv[half:, :half] = -dot(high, dot(l_ref[half:, :half], low))

    linv_t[...] = linv[...].T

    wait_bytes(ubuf, recv_t)
    mine = pl.ds(pl.multiple_of(row * stretch, stretch), stretch)
    fsend[...] = tbuf[mine, :] + jnp.sum(ubuf[...], axis=0)

    @pl.when(jnp.logical_not(fixed))
    def _():
        wait_bytes(sbuf, recv_s)

    wsend[...] += 2.0 * tdot(fsend[...], sbuf[...])

    direct = count * 8 <= width
    group = count if direct else ncols
    place = me if direct else col
    piece = width // group

    def device_of(q):
        return (q // ncols, lax.rem(q, ncols)) if direct else (row, q)

    def scatter(k, carry):
        q = lax.rem(place + k, group)
        part = pl.ds(pl.multiple_of(q * piece, piece), piece)

        def send(columns):
            pltpu.make_async_remote_copy(
                src_ref=wsend.at[part, :columns],
                dst_ref=wrecv.at[k - 1, :, :columns],
                send_sem=send_w,
                recv_sem=recv_w,
                device_id=device_of(q),
                device_id_type=MESH,
            ).start()

        pl.when(q < group // 2)(lambda: send(half))
        pl.when(q >= group // 2)(lambda: send(width))
        return carry

    lax.fori_loop(1, group, scatter, 0)

    @pl.when(jnp.logical_not(fixed))
    def _():
        pltpu.make_async_remote_copy(
            src_ref=fsend, dst_ref=fbuf, send_sem=send_f, recv_sem=recv_f,
            device_id=(owner // ncols, lax.rem(owner, ncols)), device_id_type=MESH,
        ).start()

    @pl.when(fixed)
    def _():
        fbuf[...] = fsend[...]

    mine = pl.ds(pl.multiple_of(place * piece, piece), piece)
    upper = place < group // 2

    def others(semaphore):
        rows = width + half
        pl.when(upper)(lambda: wait_bytes(pbuf.at[: rows - piece, :half], semaphore))
        pl.when(jnp.logical_not(upper))(
            lambda: wait_bytes(pbuf.at[: rows - 2 * piece, :half], semaphore)
        )

    pl.when(upper)(lambda: wait_bytes(wrecv.at[:, :, :half], recv_w))
    pl.when(jnp.logical_not(upper))(lambda: wait_bytes(wrecv, recv_w))
    total = wsend[mine, :] + jnp.sum(wrecv[...], axis=0)
    if not direct:
        ebuf[row] = total

        def exchange(k, carry):
            pltpu.make_async_remote_copy(
                src_ref=ebuf.at[row],
                dst_ref=ebuf.at[row],
                send_sem=send_e,
                recv_sem=recv_e,
                device_id=(lax.rem(row + k, nrows), col),
                device_id_type=MESH,
            ).start()
            return carry

        lax.fori_loop(1, nrows, exchange, 0)
        wait_bytes(ebuf.at[pl.ds(0, nrows - 1)], recv_e)
        total = jnp.sum(ebuf[...], axis=0)
    wfull[mine, :] = total

    paired = direct and nrows % 4 == 0
    side, spread = lax.rem(row, 2), group // 2 if paired else group

    def target(k):
        if not paired:
            return device_of(lax.rem(place + k, group))
        q = lax.rem((row // 2) * ncols + col + k, spread)
        return 2 * (q // ncols) + side, lax.rem(q, ncols)

    def gather(k, carry):
        def send(columns):
            pltpu.make_async_remote_copy(
                src_ref=wfull.at[mine, :columns],
                dst_ref=wfull.at[mine, :columns],
                send_sem=send_g,
                recv_sem=recv_g,
                device_id=target(k),
                device_id_type=MESH,
            ).start()

        pl.when(upper)(lambda: send(half))
        pl.when(jnp.logical_not(upper))(lambda: send(width))
        return carry

    lax.fori_loop(1, spread, gather, 0)

    if paired:
        rows = 3 * width // 4
        pl.when(upper)(lambda: wait_bytes(pbuf.at[: rows - piece, :half], recv_g))
        pl.when(jnp.logical_not(upper))(
            lambda: wait_bytes(pbuf.at[: rows - 2 * piece, :half], recv_g)
        )
        band = ncols * piece
        for q in range(nrows // 2):
            part = pl.ds(pl.multiple_of((2 * q + side) * band, band), band)
            columns = half if q < nrows // 4 else width
            pltpu.make_async_remote_copy(
                src_ref=wfull.at[part, :columns],
                dst_ref=wfull.at[part, :columns],
                send_sem=send_e,
                recv_sem=recv_e,
                device_id=(row + 1 - 2 * side, col),
                device_id_type=MESH,
            ).start()

    @pl.when(jnp.logical_not(fixed))
    def _():
        wait_bytes(fbuf, recv_f)

    x_ref[...] = dot(pa_ref[...] - 2.0 * fbuf[...], linv[...])

    if paired:
        wait_bytes(pbuf.at[: 3 * width // 4, :half], recv_e)
    else:
        others(recv_g)
    wfull[:half, half:] = jnp.zeros((half, half), jnp.float32)
    w = wfull[...]
    i, j = iotas(w.shape)
    lower = jnp.where(i > j, w, jnp.where(i == j, 0.5 * w, 0.0))
    symmetric = lower + lower.T
    inverse = split(linv[...])
    right = dot_parts(split(symmetric), inverse)
    k_ref[...] = 0.5 * dot_parts(split(linv_t[...]), split(right))

    wait_bytes(pbuf.at[pl.ds(0, (ncols - 1) * stretch)], send_p)
    wait_bytes(ubuf, send_t)

    @pl.when(jnp.logical_not(fixed))
    def _():
        wait_bytes(sbuf, send_s)
        wait_bytes(fbuf, send_f)

    others(send_w)
    pl.when(upper)(lambda: wait_bytes(wrecv.at[: spread - 1, :, :half], send_g))
    pl.when(jnp.logical_not(upper))(lambda: wait_bytes(wrecv.at[: spread - 1], send_g))
    if paired:
        wait_bytes(pbuf.at[: 3 * width // 4, :half], send_e)
    if not direct:
        wait_bytes(ebuf.at[pl.ds(0, nrows - 1)], send_e)


def body(trailing_adjoint, panel, panel_adjoint, diag_factor, diag_adjoint):
    nrows, ncols = lax.axis_size("row"), lax.axis_size("col")
    stretch, width = panel.shape
    group = nrows * ncols if nrows * ncols * 8 <= width else ncols
    piece = width // group
    vmem = lambda *shape: pltpu.VMEM(shape, jnp.float32)
    return pl.pallas_call(
        functools.partial(kernel, nrows, ncols),
        out_shape=(
            jax.ShapeDtypeStruct(panel.shape, jnp.float32),
            jax.ShapeDtypeStruct(diag_factor.shape, jnp.float32),
        ),
        in_specs=[pl.BlockSpec(memory_space=pltpu.VMEM)] * 5,
        out_specs=(pl.BlockSpec(memory_space=pltpu.VMEM),) * 2,
        scratch_shapes=[
            vmem(ncols * stretch, width),
            vmem(nrows * stretch, width),
            vmem(nrows - 1, stretch, width),
            vmem(stretch, width),
            vmem(stretch, width),
            vmem(stretch, width),
            vmem(width, width),
            vmem(group - 1, piece, width),
            vmem(width, width),
            vmem(nrows, piece, width),
            vmem(width, width),
            vmem(width, width),
        ]
        + [pltpu.SemaphoreType.DMA, pltpu.SemaphoreType.DMA((ncols // 2,))]
        + [pltpu.SemaphoreType.DMA] * 13,
        compiler_params=pltpu.CompilerParams(
            collective_id=0, has_side_effects=True, vmem_limit_bytes=40 * 1024 * 1024
        ),
    )(trailing_adjoint.T, panel, panel_adjoint, diag_factor, diag_adjoint.T)


def solution(mesh):
    return jax.shard_map(
        body,
        mesh=mesh,
        in_specs=(
            P("row", "col"),
            P(("row", "col"), None),
            P(("row", "col"), None),
            P(),
            P("row", "col"),
        ),
        out_specs=(P(("row", "col"), None), P()),
        check_vma=False,
    )
```

```python
import functools

import jax
import jax.numpy as jnp
from jax import lax
from jax.experimental import pallas as pl
from jax.experimental.pallas import tpu as pltpu
from jax.sharding import PartitionSpec as P

MESH = pl.DeviceIdType.MESH
HIGHEST = lax.Precision.HIGHEST
CHUNK = 384


def split(x):
    high = x.astype(jnp.bfloat16)
    return high, (x - high.astype(jnp.float32)).astype(jnp.bfloat16)


def one(a, b):
    return jnp.dot(a, b, preferred_element_type=jnp.float32)


def dot_parts(a, b):
    return one(a[0], b[0]) + (one(a[0], b[1]) + one(a[1], b[0]))


def dot(a, b):
    return dot_parts(split(a), split(b))


def tdot(a, b):
    return dot(a.T, b)


def exact_dot(a, b):
    return jnp.dot(a, b, precision=HIGHEST, preferred_element_type=jnp.float32)


def iotas(shape):
    return (
        lax.broadcasted_iota(jnp.int32, shape, 0),
        lax.broadcasted_iota(jnp.int32, shape, 1),
    )


def inverse_pair(first, second):
    size = first.shape[0]
    i, j = iotas(first.shape)
    blocks, inverses = (first, second), []
    for block in blocks:
        diagonal = jnp.where(i == j, block, 0.0)
        down = 1.0 / jnp.sum(diagonal, axis=1, keepdims=True)
        across = 1.0 / jnp.sum(diagonal, axis=0, keepdims=True)
        pair = ((i >> 1) == (j >> 1)) & (i > j)
        inverses.append(
            jnp.where(i == j, jnp.broadcast_to(down, block.shape), 0.0)
            - jnp.where(pair, block, 0.0) * down * across
        )
    level = 1
    while (1 << level) < size:
        below = ((i >> (level + 1)) == (j >> (level + 1))) & ((i >> level) > (j >> level))
        halves = [dot(x, jnp.where(below, block, 0.0)) for x, block in zip(inverses, blocks)]
        inverses = [x - dot(half, x) for x, half in zip(inverses, halves)]
        level += 1
    return inverses


def wait_bytes(ref, semaphore):
    pltpu.make_async_copy(ref, ref, semaphore).wait()


def kernel(
    nrows, ncols, a_ref, p_ref, pa_ref, l_ref, d_ref, x_ref, k_ref,
    pbuf, tbuf, ubuf, sbuf, fsend, fbuf, wsend, wrecv, wfull, ebuf, linv, linv_t,
    send_p, recv_row, recv_col, send_t, recv_t, send_w, recv_w, send_g, recv_g, send_e, recv_e,
    send_s, recv_s, send_f, recv_f,
):
    row, col = lax.axis_index("row"), lax.axis_index("col")
    count = nrows * ncols
    me = row * ncols + col
    stretch, width = p_ref.shape
    half = width // 2

    barrier = pltpu.get_barrier_semaphore()

    def greet(k, carry):
        peer = lax.rem(me + k, count)
        pl.semaphore_signal(
            barrier, inc=1, device_id=(peer // ncols, lax.rem(peer, ncols)), device_id_type=MESH
        )
        return carry

    lax.fori_loop(1, count, greet, 0)

    i, j = iotas((d_ref.shape[0], width))
    placed = tdot(d_ref[...], jnp.where(j == i + col * d_ref.shape[0], 1.0, 0.0))
    drows = d_ref.shape[1]
    lrows = l_ref[pl.ds(pl.multiple_of(row * drows, drows), drows), :]
    wsend[...] = tdot(lrows, placed) - tdot(pa_ref[...], p_ref[...])
    pbuf[pl.ds(pl.multiple_of(col * stretch, stretch), stretch), :] = p_ref[...]

    pl.semaphore_wait(barrier, count - 1)

    shard = pl.ds(pl.multiple_of(col * stretch, stretch), stretch)
    fours = ncols // 2
    place_c, parity = col // 2, lax.rem(col, 2)
    neighbour = 2 * place_c + 1 - parity
    summer = (lax.rem(me, nrows), me // nrows)
    owner = nrows * col + row
    fixed = owner == me

    def to_row(k, carry):
        pltpu.make_async_remote_copy(
            src_ref=p_ref,
            dst_ref=pbuf.at[shard],
            send_sem=send_p,
            recv_sem=recv_row.at[k],
            device_id=(row, 2 * lax.rem(place_c + k, fours) + parity),
            device_id_type=MESH,
        ).start()
        return carry

    lax.fori_loop(1, fours, to_row, 0)
    pltpu.make_async_remote_copy(
        src_ref=p_ref, dst_ref=pbuf.at[shard], send_sem=send_p, recv_sem=recv_col,
        device_id=(row, neighbour), device_id_type=MESH,
    ).start()

    def hand_on(k, carry):
        origin = 2 * lax.rem(place_c + fours - k, fours) + parity
        arrived = pbuf.at[pl.ds(pl.multiple_of(origin * stretch, stretch), stretch)]
        wait_bytes(arrived, recv_row.at[k])
        pltpu.make_async_remote_copy(
            src_ref=arrived, dst_ref=arrived, send_sem=send_p, recv_sem=recv_col,
            device_id=(row, neighbour), device_id_type=MESH,
        ).start()
        return carry

    lax.fori_loop(1, fours, hand_on, 0)

    @pl.when(jnp.logical_not(fixed))
    def _():
        pltpu.make_async_remote_copy(
            src_ref=p_ref, dst_ref=sbuf, send_sem=send_s, recv_sem=recv_s,
            device_id=summer, device_id_type=MESH,
        ).start()

    @pl.when(fixed)
    def _():
        sbuf[...] = p_ref[...]

    wait_bytes(pbuf.at[pl.ds(0, fours * stretch)], recv_col)
    rows = a_ref.shape[1]
    tbuf[...] = dot(a_ref[:, :CHUNK], pbuf[:CHUNK, :])
    if rows > CHUNK:

        def add_chunk(k, carry):
            part = pl.ds(pl.multiple_of(k * CHUNK, CHUNK), CHUNK)
            tbuf[...] += dot(a_ref[:, part], pbuf[part, :])
            return carry

        lax.fori_loop(1, rows // CHUNK, add_chunk, 0)

    def to_summer(k, carry):
        q = lax.rem(row + k, nrows)
        pltpu.make_async_remote_copy(
            src_ref=tbuf.at[pl.ds(pl.multiple_of(q * stretch, stretch), stretch)],
            dst_ref=ubuf.at[k - 1],
            send_sem=send_t,
            recv_sem=recv_t,
            device_id=(q, col),
            device_id_type=MESH,
        ).start()
        return carry

    lax.fori_loop(1, nrows, to_summer, 0)
    low, high = inverse_pair(l_ref[:half, :half], l_ref[half:, half:])
    linv[:half, :half] = low
    linv[:half, half:] = jnp.zeros((half, half), jnp.float32)
    linv[half:, half:] = high
    linv[half:, :half] = -dot(high, dot(l_ref[half:, :half], low))

    linv_t[...] = linv[...].T

    wait_bytes(ubuf, recv_t)
    mine = pl.ds(pl.multiple_of(row * stretch, stretch), stretch)
    fsend[...] = tbuf[mine, :] + jnp.sum(ubuf[...], axis=0)

    @pl.when(jnp.logical_not(fixed))
    def _():
        wait_bytes(sbuf, recv_s)

    wsend[...] += 2.0 * tdot(fsend[...], sbuf[...])

    direct = count * 8 <= width
    group = count if direct else ncols
    place = me if direct else col
    piece = width // group

    def device_of(q):
        return (q // ncols, lax.rem(q, ncols)) if direct else (row, q)

    def scatter(k, carry):
        q = lax.rem(place + k, group)
        part = pl.ds(pl.multiple_of(q * piece, piece), piece)

        def send(columns):
            pltpu.make_async_remote_copy(
                src_ref=wsend.at[part, :columns],
                dst_ref=wrecv.at[k - 1, :, :columns],
                send_sem=send_w,
                recv_sem=recv_w,
                device_id=device_of(q),
                device_id_type=MESH,
            ).start()

        pl.when(q < group // 2)(lambda: send(half))
        pl.when(q >= group // 2)(lambda: send(width))
        return carry

    lax.fori_loop(1, group, scatter, 0)

    @pl.when(jnp.logical_not(fixed))
    def _():
        pltpu.make_async_remote_copy(
            src_ref=fsend, dst_ref=fbuf, send_sem=send_f, recv_sem=recv_f,
            device_id=(owner // ncols, lax.rem(owner, ncols)), device_id_type=MESH,
        ).start()

    @pl.when(fixed)
    def _():
        fbuf[...] = fsend[...]

    mine = pl.ds(pl.multiple_of(place * piece, piece), piece)
    upper = place < group // 2

    def others(semaphore):
        rows = width + half
        pl.when(upper)(lambda: wait_bytes(pbuf.at[: rows - piece, :half], semaphore))
        pl.when(jnp.logical_not(upper))(
            lambda: wait_bytes(pbuf.at[: rows - 2 * piece, :half], semaphore)
        )

    pl.when(upper)(lambda: wait_bytes(wrecv.at[:, :, :half], recv_w))
    pl.when(jnp.logical_not(upper))(lambda: wait_bytes(wrecv, recv_w))
    total = wsend[mine, :] + jnp.sum(wrecv[...], axis=0)
    if not direct:
        ebuf[row] = total

        def exchange(k, carry):
            pltpu.make_async_remote_copy(
                src_ref=ebuf.at[row],
                dst_ref=ebuf.at[row],
                send_sem=send_e,
                recv_sem=recv_e,
                device_id=(lax.rem(row + k, nrows), col),
                device_id_type=MESH,
            ).start()
            return carry

        lax.fori_loop(1, nrows, exchange, 0)
        wait_bytes(ebuf.at[pl.ds(0, nrows - 1)], recv_e)
        total = jnp.sum(ebuf[...], axis=0)
    wfull[mine, :] = total

    paired = direct and nrows % 4 == 0
    side, spread = lax.rem(row, 2), group // 2 if paired else group

    def target(k):
        if not paired:
            return device_of(lax.rem(place + k, group))
        q = lax.rem((row // 2) * ncols + col + k, spread)
        return 2 * (q // ncols) + side, lax.rem(q, ncols)

    def gather(k, carry):
        def send(columns):
            pltpu.make_async_remote_copy(
                src_ref=wfull.at[mine, :columns],
                dst_ref=wfull.at[mine, :columns],
                send_sem=send_g,
                recv_sem=recv_g,
                device_id=target(k),
                device_id_type=MESH,
            ).start()

        pl.when(upper)(lambda: send(half))
        pl.when(jnp.logical_not(upper))(lambda: send(width))
        return carry

    lax.fori_loop(1, spread, gather, 0)

    if paired:
        rows = 3 * width // 4
        pl.when(upper)(lambda: wait_bytes(pbuf.at[: rows - piece, :half], recv_g))
        pl.when(jnp.logical_not(upper))(
            lambda: wait_bytes(pbuf.at[: rows - 2 * piece, :half], recv_g)
        )
        band = ncols * piece
        for q in range(nrows // 2):
            part = pl.ds(pl.multiple_of((2 * q + side) * band, band), band)
            columns = half if q < nrows // 4 else width
            pltpu.make_async_remote_copy(
                src_ref=wfull.at[part, :columns],
                dst_ref=wfull.at[part, :columns],
                send_sem=send_e,
                recv_sem=recv_e,
                device_id=(row + 1 - 2 * side, col),
                device_id_type=MESH,
            ).start()

    @pl.when(jnp.logical_not(fixed))
    def _():
        wait_bytes(fbuf, recv_f)

    x_ref[...] = dot(pa_ref[...] - 2.0 * fbuf[...], linv[...])

    inverse, inverse_t = split(linv[...]), split(linv_t[...])
    if paired:
        wait_bytes(pbuf.at[: 3 * width // 4, :half], recv_e)
    else:
        others(recv_g)
    wfull[:half, half:] = jnp.zeros((half, half), jnp.float32)
    w = wfull[...]
    i, j = iotas(w.shape)
    lower = jnp.where(i > j, w, jnp.where(i == j, 0.5 * w, 0.0))
    symmetric = lower + lower.T
    right = dot_parts(split(symmetric), inverse)
    k_ref[...] = 0.5 * dot_parts(inverse_t, split(right))

    wait_bytes(pbuf.at[pl.ds(0, (ncols - 1) * stretch)], send_p)
    wait_bytes(ubuf, send_t)

    @pl.when(jnp.logical_not(fixed))
    def _():
        wait_bytes(sbuf, send_s)
        wait_bytes(fbuf, send_f)

    others(send_w)
    pl.when(upper)(lambda: wait_bytes(wrecv.at[: spread - 1, :, :half], send_g))
    pl.when(jnp.logical_not(upper))(lambda: wait_bytes(wrecv.at[: spread - 1], send_g))
    if paired:
        wait_bytes(pbuf.at[: 3 * width // 4, :half], send_e)
    if not direct:
        wait_bytes(ebuf.at[pl.ds(0, nrows - 1)], send_e)


def body(trailing_adjoint, panel, panel_adjoint, diag_factor, diag_adjoint):
    nrows, ncols = lax.axis_size("row"), lax.axis_size("col")
    stretch, width = panel.shape
    group = nrows * ncols if nrows * ncols * 8 <= width else ncols
    piece = width // group
    vmem = lambda *shape: pltpu.VMEM(shape, jnp.float32)
    return pl.pallas_call(
        functools.partial(kernel, nrows, ncols),
        out_shape=(
            jax.ShapeDtypeStruct(panel.shape, jnp.float32),
            jax.ShapeDtypeStruct(diag_factor.shape, jnp.float32),
        ),
        in_specs=[pl.BlockSpec(memory_space=pltpu.VMEM)] * 5,
        out_specs=(pl.BlockSpec(memory_space=pltpu.VMEM),) * 2,
        scratch_shapes=[
            vmem(ncols * stretch, width),
            vmem(nrows * stretch, width),
            vmem(nrows - 1, stretch, width),
            vmem(stretch, width),
            vmem(stretch, width),
            vmem(stretch, width),
            vmem(width, width),
            vmem(group - 1, piece, width),
            vmem(width, width),
            vmem(nrows, piece, width),
            vmem(width, width),
            vmem(width, width),
        ]
        + [pltpu.SemaphoreType.DMA, pltpu.SemaphoreType.DMA((ncols // 2,))]
        + [pltpu.SemaphoreType.DMA] * 13,
        compiler_params=pltpu.CompilerParams(
            collective_id=0, has_side_effects=True, vmem_limit_bytes=40 * 1024 * 1024
        ),
    )(trailing_adjoint.T, panel, panel_adjoint, diag_factor, diag_adjoint.T)


def solution(mesh):
    return jax.shard_map(
        body,
        mesh=mesh,
        in_specs=(
            P("row", "col"),
            P(("row", "col"), None),
            P(("row", "col"), None),
            P(),
            P("row", "col"),
        ),
        out_specs=(P(("row", "col"), None), P()),
        check_vma=False,
    )
```
